256 devices in a mesh: tm: 4 (over x_lo, core), space: 64 (over z, y, x_hi).
Axes of the slice: x: 4 (x_hi: 2, x_lo: 2; x = x_hi * 2 + x_lo), y: 4, z: 8, core: 2. Of those that a mesh axis runs over, the one named last changes fastest.
Arguments:
- adjoint_end: float32 [8, 16384, 1024], P('tm', 'space'), may hold values from -6 to 6
- adjoint_source: float32 [8, 2, 16384, 1024], P('tm', None, 'space'), may hold values from -6 to 6
- region: int32 [16384, 1024], P('space'), may hold values from 0 to 7
- dirichlet: int32 [16384, 1024], P('space'), may hold values 0 or 1
- reluctivity: float32 [8], replicated, may hold values from 0.5 to 8
- conductance: float32 [8], replicated, may hold values from 0 to 2
Outputs:
- new_end: float32 [8, 16384, 1024], P('tm', 'space')
The draws below stay inside these ranges and needn't reach their ends.
All inputs are finite; a program needn't handle non-finite values. No bound on the sum of `dirichlet` on one device may be relied on, other than what follows from the above.
Results may differ from the reference program's by a relative error of at most 0.00002.
Values sent between devices are 32-bit elements; how exact they have to be, the bound alone decides.
No kernel may reach another device: no remote copies, remote signals or barrier semaphores. Data moves between devices by JAX's collectives and lax.ppermute only.
A program may use at most 128 MiB of HBM per device.

```python
import math
import jax
import jax.numpy as jnp
from jax import lax

NR = 1024
STEPS = 2
SWEEPS = 2
REGIONS = 8
SLICES = 8
NTH = 16384


def set_ends(values, own_key, low, top_value):
    place = [jax.random.randint(jax.random.fold_in(own_key, axis), (), 0, length) for axis, length in enumerate(values.shape)]
    main_axis = values.shape.index(max(values.shape))
    neighbour = place[:main_axis] + [(place[main_axis] + 1) % values.shape[main_axis]] + place[main_axis + 1:]
    return values.at[tuple(place)].set(low).at[tuple(neighbour)].set(top_value)


def levels(key, shape, cuts, smallest, high):
    def one(axis_at, parts):
        heights = jax.random.uniform(jax.random.fold_in(jax.random.fold_in(key, 6), axis_at), (parts,), jnp.float32, smallest / len(cuts), high / len(cuts))
        return jnp.repeat(jnp.exp(heights), shape[axis_at] // parts).reshape((-1,) + (1,) * (len(shape) - axis_at - 1))

    gain = one(*cuts[0])
    for cut in cuts[1:]:
        gain = gain * one(*cut)
    return gain


def normal_values(own_key, shape, scale, most, shards=(), kind=jnp.bfloat16):
    entries = scale * jax.random.normal(own_key, shape, jnp.float32)
    if shards:
        entries = entries * levels(own_key, shape, shards, -0.22, 0.18)
    return jnp.clip(entries, -most, most).astype(kind)


def setup_inputs(seed: int = 0) -> dict:
    streams_of = jax.random.split(jax.random.key(seed), 7)
    adjoint_end = normal_values(streams_of[0], (SLICES, NTH, NR), 1.0, 6.0, ((0, 4), (1, 64)), jnp.float32)
    adjoint_source = normal_values(streams_of[1], (SLICES, STEPS, NTH, NR), 1.0, 6.0, ((0, 4), (2, 64)), jnp.float32)
    region = set_ends(jax.random.randint(streams_of[2], (NTH, NR), 0, REGIONS), jax.random.fold_in(streams_of[2], 1), 0, REGIONS - 1).astype(jnp.int32)
    dirichlet = set_ends((jax.random.randint(streams_of[3], (NTH, NR), 0, 8) < 1).astype(jnp.int32), jax.random.fold_in(streams_of[3], 1), 0, 1)
    reluctivity = jnp.clip(jnp.exp(jax.random.uniform(streams_of[4], (REGIONS,), jnp.float32, math.log(0.5), math.log(8.0))), 0.5, 8.0)
    conductance = jnp.clip(jax.random.uniform(streams_of[5], (REGIONS,), jnp.float32, 0.0, 2.0), 0.0, 2.0)
    return dict(adjoint_end=adjoint_end, adjoint_source=adjoint_source, region=region, dirichlet=dirichlet, reluctivity=reluctivity, conductance=conductance)


relaxation = 0.8


def lookup(region, table):
    result = jnp.zeros(region.shape, table.dtype)
    for entry in range(table.shape[0]):
        result = jnp.where(region == entry, table[entry], result)
    return result


def wrap_pad(array, width):
    return jnp.concatenate([array[..., -width:, :], array, array[..., :width, :]], axis=-2)


def face_weights(reluct_pad, mass_term, spacing):
    radial = reluct_pad.shape[-1]
    position = jnp.arange(radial, dtype=jnp.float32)
    cycle_factor = 1.0 + position * spacing
    outer_factor = 1.0 + (position + 0.5) * spacing
    inner_factor = 1.0 + (position - 0.5) * spacing
    centre = reluct_pad[1:-1]
    west_face = 0.5 * (centre + reluct_pad[:-2]) / cycle_factor
    east_face = 0.5 * (centre + reluct_pad[2:]) / cycle_factor
    upward = jnp.concatenate([centre[:, 1:], centre[:, -1:]], axis=1)
    downward = jnp.concatenate([centre[:, :1], centre[:, :-1]], axis=1)
    outer_face = 0.5 * (centre + upward) * outer_factor
    inner_face = 0.5 * (centre + downward) * inner_factor
    diagonal = mass_term + west_face + east_face + outer_face + inner_face
    return (west_face, east_face, outer_face, inner_face, diagonal, relaxation / diagonal)


def smooth_once(padded, right_side, weights, keep_mask):
    west_face, east_face, outer_face, inner_face, diagonal, gain_step = weights
    centre = padded[:, 1:-1]
    edge_zeros = jnp.zeros_like(centre[..., :1])
    upward = jnp.concatenate([centre[..., 1:], edge_zeros], axis=-1)
    downward = jnp.concatenate([edge_zeros, centre[..., :-1]], axis=-1)
    applied = diagonal * centre - west_face * padded[:, :-2] - east_face * padded[:, 2:] - outer_face * upward - inner_face * downward
    return keep_mask * (centre + gain_step * (right_side - applied))


def reference(adjoint_end, adjoint_source, region, dirichlet, reluctivity, conductance):
    columns = adjoint_end.shape[1]
    radial = adjoint_end.shape[2]
    spacing = 2.0 * math.pi / columns
    position = jnp.arange(radial, dtype=jnp.float32)
    reluct = lookup(region, reluctivity)
    mass_term = lookup(region, conductance) * (1.0 + position * spacing)
    keep_mask = (1 - dirichlet).astype(jnp.float32)
    weights = face_weights(wrap_pad(reluct, 1), mass_term, spacing)

    def one_slice(pair):
        state, sources = pair
        state = state[None]
        for step_index in range(STEPS):
            right_side = mass_term * state + sources[step_index][None]
            for sweep_index in range(SWEEPS):
                state = smooth_once(wrap_pad(state, 1), right_side, weights, keep_mask)
        return state[0]

    starts = lax.map(one_slice, (adjoint_end, adjoint_source))
    return jnp.concatenate([starts[1:], starts[:1]], axis=0)
```

```python
import functools
import math

import jax
import jax.numpy as jnp
from jax import lax
from jax.experimental import pallas as pl
from jax.experimental.pallas import tpu as pltpu
from jax.sharding import PartitionSpec as P

RELAX = 0.8
KEEP_SHARE = 0.2
F32 = jnp.float32
ANY = pl.BlockSpec(memory_space=pltpu.HBM)
VMEM = pl.BlockSpec(memory_space=pltpu.VMEM)
SMEM = pl.BlockSpec(memory_space=pltpu.SMEM)
PLANES = 7
LOOK, MAKE, GO = 9, 3, 9


def tables(region, *names):
    low = (region & 1) != 0
    mid = (region & 2) != 0
    top = (region & 4) != 0
    found = []
    for t in names:
        pairs = [jnp.where(low, t[2 * k + 1], t[2 * k]) for k in range(4)]
        halves = [jnp.where(mid, pairs[2 * k + 1], pairs[2 * k]) for k in range(2)]
        found.append(jnp.where(top, halves[1], halves[0]))
    return found


def row_factors(rows, radial, spacing):
    lane = lax.broadcasted_iota(jnp.int32, (rows, radial), 1)
    position = lane.astype(F32)
    cycle = 1.0 + position * spacing
    outer = 0.5 * (1.0 + (position + 0.5) * spacing)
    inner = 0.5 * (1.0 + (position - 0.5) * spacing)
    return lane, cycle, 0.5 / cycle, outer, inner


def weight_planes(rho, rho_west, rho_east, cond, dirichlet, factors):
    lane, cycle, half_cycle, outer_f, inner_f = factors
    radial = rho.shape[1]
    first, final = lane == 0, lane == radial - 1
    up = jnp.where(final, rho, pltpu.roll(rho, radial - 1, 1))
    down = jnp.where(first, rho, pltpu.roll(rho, 1, 1))
    west = (rho + rho_west) * half_cycle
    east = (rho + rho_east) * half_cycle
    outer = (rho + up) * outer_f
    inner = (rho + down) * inner_f
    mass = cond * cycle
    diagonal = mass + west + east + outer + inner
    free = dirichlet == 0
    gain = jnp.where(free, RELAX / diagonal, 0.0)
    own = jnp.where(free, KEEP_SHARE, 0.0)
    outer_gain = jnp.where(final, 0.0, gain * outer)
    inner_gain = jnp.where(first, 0.0, gain * inner)
    return own, gain * west, gain * east, outer_gain, inner_gain, gain, gain * mass


def stencil(centre, west, east, w, right):
    radial = centre.shape[1]
    up = pltpu.roll(centre, radial - 1, 1)
    down = pltpu.roll(centre, 1, 1)
    return (w[0] * centre + w[1] * west) + (w[2] * east + w[3] * up) + (w[4] * down + right)


def copy_in(src, dst, sem):
    return pltpu.make_async_copy(src, dst, sem)


def each(lo, hi, work, group):
    group = min(group, hi - lo)
    groups = -(-(hi - lo) // group)

    def step(k, _):
        at = jnp.minimum(lo + k * group, hi - group)
        work([at + m for m in range(group)])
        return 0

    lax.fori_loop(0, groups, step, 0)


def beside(x, t, sub):
    c = x[t + 1]
    west = jnp.where(sub == 0, x[t, 7:8, :], pltpu.roll(c, 1, 0))
    east = jnp.where(sub == 7, x[t + 2, 0:1, :], pltpu.roll(c, 7, 0))
    return c, west, east


def weights_loop(reg, diri, rho_s, cond_s, fac, w_out, rho_tab, cond_tab, tiles):
    radial = reg.shape[2]

    def look(ts):
        found = [tables(reg[t], rho_tab, cond_tab) for t in ts]
        for t, (r, c) in zip(ts, found):
            rho_s[t + 1] = r
            cond_s[t] = c

    each(0, tiles, look, LOOK)
    lane = lax.broadcasted_iota(jnp.int32, (8, radial), 1)
    sub = lax.broadcasted_iota(jnp.int32, (8, radial), 0)

    def make(ts):
        seen = [beside(rho_s, t, sub) + (cond_s[t], diri[t]) for t in ts]
        planes = [weight_planes(*v, (lane, fac[0], fac[1], fac[2], fac[3])) for v in seen]
        for t, w in zip(ts, planes):
            for k in range(PLANES):
                w_out[k, t] = w[k]

    each(0, tiles, make, MAKE)


def sweep(x, y, w, w_at, src, right, first, lo, hi, y_at=1):
    sub = lax.broadcasted_iota(jnp.int32, x.shape[1:], 0)

    def go(ts):
        seen = [beside(x, t, sub) for t in ts]
        rights, news = [], []
        for t, (c, west, east) in zip(ts, seen):
            if first:
                b = w[5, t - w_at] * src[t] + w[6, t - w_at] * c
            else:
                b = right[t]
            rights.append(b)
            news.append(stencil(c, west, east, [w[k, t - w_at] for k in range(5)], b))
        for t, b, new in zip(ts, rights, news):
            if first:
                right[t] = b
            y[t + y_at] = new

    each(lo, hi, go, GO)


def edge_loads(end, source, region, diri, at, buf, regs, sems):
    return [
        copy_in(end.at[1, at], buf.at[0], sems.at[0]),
        copy_in(source.at[1, 0, at], buf.at[1], sems.at[1]),
        copy_in(source.at[1, 1, at], buf.at[2], sems.at[2]),
        copy_in(end.at[0, at], buf.at[3], sems.at[3]),
        copy_in(source.at[0, 0, at], buf.at[4], sems.at[4]),
        copy_in(source.at[0, 1, at], buf.at[5], sems.at[5]),
        copy_in(region.at[at], regs.at[0], sems.at[6]),
        copy_in(diri.at[at], regs.at[1], sems.at[7]),
    ]


def write_packs(buf, regs, a, b, side):
    pick = (lambda m: slice(0, m)) if side == 0 else (lambda m: slice(8 - m, 8))
    for out, at in ((a, 0), (b, 3)):
        out[0:4, :] = buf[at, pick(4), :]
        out[4:7, :] = buf[at + 1, pick(3), :]
        out[7:8, :] = buf[at + 2, pick(1), :]
    a[8:12, :] = regs[0, pick(4), :].astype(F32)
    a[12:15, :] = regs[1, pick(3), :].astype(F32)
    a[15:16, :] = jnp.zeros((1, a.shape[1]), F32)


def pack_kernel(end, source, region, diri, up_a, up_b, own, buf, regs, sems):
    last = end.shape[1] - 1
    copies = edge_loads(end, source, region, diri, last, buf, regs, sems)
    copies += [
        copy_in(end.at[0, 0], own.at[0], sems.at[8]),
        copy_in(source.at[0, 0, 0], own.at[1], sems.at[9]),
        copy_in(source.at[0, 1, 0], own.at[2], sems.at[10]),
    ]
    for c in copies:
        c.start()
    for c in copies:
        c.wait()
    write_packs(buf, regs, up_a, up_b, 1)
    for k in range(3):
        own[3 + k] = buf[3 + k]


def chunk_kernel(base, tiles, lo, hi, spacing, rho_tab, cond_tab, end, source, region, diri, _, *refs):
    w_out, chunk = refs[:2]
    packs = refs[2:-13]
    reg_v, dir_v, x, y, s0, s1, right, rho_s, cond_s, fac, rt, ct, sems = refs[-13:]
    if packs:
        *packs, buf, regs, edge_sems = packs
    radial = end.shape[3]
    rows = pl.ds(base, tiles)
    copies = [
        copy_in(rho_tab, rt, sems.at[0]),
        copy_in(cond_tab, ct, sems.at[1]),
        copy_in(region.at[rows], reg_v, sems.at[2]),
        copy_in(diri.at[rows], dir_v, sems.at[3]),
        copy_in(end.at[0, rows], x.at[pl.ds(1, tiles)], sems.at[4]),
        copy_in(source.at[0, 0, rows], s0, sems.at[5]),
        copy_in(source.at[0, 1, rows], s1, sems.at[6]),
    ]
    for c in copies:
        c.start()
    if packs:
        edges = edge_loads(end, source, region, diri, 0, buf, regs, edge_sems)
        for c in edges:
            c.start()
    _, cycle, half, outer, inner = row_factors(8, radial, spacing)
    for k, f in enumerate((cycle, half, outer, inner)):
        fac[k] = f
    for c in copies[:4]:
        c.wait()
    rts = [rt[k] for k in range(8)]
    cts = [ct[k] for k in range(8)]
    weights_loop(reg_v, dir_v, rho_s, cond_s, fac, w_out, rts, cts, tiles)
    copies[4].wait()
    copies[5].wait()
    sweep(x, y, w_out, 0, s0, right, True, 0, tiles)
    sweep(y, x, w_out, 0, None, right, False, 0, tiles)
    copies[6].wait()
    sweep(x, y, w_out, 0, s1, right, True, 0, tiles)
    sweep(y, chunk, w_out, 0, None, right, False, lo, hi, -lo)
    if packs:
        for c in edges:
            c.wait()
        write_packs(buf, regs, packs[0], packs[1], 0)


def second_kernel(w1, w2, end, source, out, ends, x, y, s0, s1, right, sems):
    tiles = end.shape[1]
    half = tiles // 2
    quarter = tiles // 4

    def piece(k):
        return pl.ds(k * quarter, quarter)

    def load(k):
        return [
            copy_in(end.at[1, piece(k)], x.at[pl.ds(1 + k * quarter, quarter)], sems.at[0, k]),
            copy_in(source.at[1, 0, piece(k)], s0.at[piece(k)], sems.at[1, k]),
        ]

    def back(k):
        return copy_in(x.at[pl.ds(1 + k * quarter, quarter)], out.at[0, piece(k)], sems.at[2, k])

    late = copy_in(source.at[1, 1], s1, sems.at[3, 0])
    for k in range(4):
        for c in load(k):
            c.start()
    late.start()
    skip = tiles - w2.shape[1]

    def both(a, b, src, first, before=None, after=None):
        for k in range(4):
            if before:
                before(k)
            w, at = (w1, 0) if k < 2 else (w2, skip)
            sweep(a, b, w, at, src, right, first, k * quarter, (k + 1) * quarter)
            if after:
                after(k)

    def arrived(k):
        for p in ([0, 1] if k == 0 else [k + 1] if k < 3 else []):
            for c in load(p):
                c.wait()

    both(x, y, s0, True, arrived)
    both(y, x, None, False)
    late.wait()
    both(x, y, s1, True)
    both(y, x, None, False, None, lambda k: back(k).start())
    ends[0] = x[1]
    ends[1] = x[tiles]
    for k in range(4):
        back(k).wait()


def edge_kernel(
    side, spacing,
    rho_tab, cond_tab, end, source, region, diri, got, bulk, ends, pa, pb, _,
    out,
    own, regs, xw, sw, rw, dw, tiles_out, rt, ct, sems,
):
    tiles, radial = end.shape[1], end.shape[3]
    half = tiles // 2
    at = side * (tiles - 1)
    moved = copy_in(
        bulk.at[pl.ds(1 - side, half - 1)], out.at[1, pl.ds(1 if side == 0 else half, half - 1)], sems.at[0]
    )
    loads = [
        copy_in(rho_tab, rt, sems.at[1]),
        copy_in(cond_tab, ct, sems.at[2]),
        copy_in(region.at[at], regs.at[0], sems.at[3]),
        copy_in(diri.at[at], regs.at[1], sems.at[4]),
        copy_in(end.at[1, at], own.at[0], sems.at[5]),
        copy_in(source.at[1, 0, at], own.at[1], sems.at[6]),
        copy_in(source.at[1, 1, at], own.at[2], sems.at[7]),
    ]
    for c in loads:
        c.start()
    moved.start()
    factors = row_factors(16, radial, spacing)
    zero = jnp.zeros((16, radial), F32)
    mine = 8 if side == 0 else 0
    halo = (lambda m: slice(8 - m, 8)) if side == 0 else (lambda m: slice(8, 8 + m))
    rw[...] = jnp.zeros((16, radial), jnp.int32)
    dw[...] = jnp.zeros((16, radial), jnp.int32)
    rw[halo(4), :] = pa[8:12, :].astype(jnp.int32)
    dw[halo(3), :] = pa[12:15, :].astype(jnp.int32)
    for p, pack in ((0, pa), (1, pb)):
        xw[p] = zero
        sw[p, 0] = zero
        sw[p, 1] = zero
        xw[p, halo(4), :] = pack[0:4, :]
        sw[p, 0, halo(3), :] = pack[4:7, :]
        sw[p, 1, halo(1), :] = pack[7:8, :]
    xw[1, mine : mine + 8, :] = got[3 * side]
    sw[1, 0, mine : mine + 8, :] = got[3 * side + 1]
    sw[1, 1, mine : mine + 8, :] = got[3 * side + 2]
    for c in loads:
        c.wait()
    rw[mine : mine + 8, :] = regs[0]
    dw[mine : mine + 8, :] = regs[1]
    xw[0, mine : mine + 8, :] = own[0]
    sw[0, 0, mine : mine + 8, :] = own[1]
    sw[0, 1, mine : mine + 8, :] = own[2]
    rho, cond = tables(rw[...], [rt[k] for k in range(8)], [ct[k] for k in range(8)])
    w = weight_planes(rho, pltpu.roll(rho, 1, 0), pltpu.roll(rho, 15, 0), cond, dw[...], factors)
    state = [xw[0], xw[1]]
    for step in range(2):
        right = [w[5] * sw[p, step] + w[6] * state[p] for p in range(2)]
        for _ in range(2):
            state = [
                stencil(v, pltpu.roll(v, 1, 0), pltpu.roll(v, 15, 0), w, r) for v, r in zip(state, right)
            ]
    sub = lax.broadcasted_iota(jnp.int32, (8, radial), 0)
    edge = sub < 4 if side == 0 else sub >= 4
    stores = []
    for p, keep in ((0, ends[side]), (1, bulk[side * (half - 1)])):
        tiles_out[p] = jnp.where(edge, state[p][mine : mine + 8, :], keep)
        stores.append(copy_in(tiles_out.at[p], out.at[p, at], sems.at[8 + p]))
        stores[-1].start()
    for c in [moved] + stores:
        c.wait()


def params(mib):
    return pltpu.CompilerParams(vmem_limit_bytes=mib * 2**20)


def cost(us):
    return pl.CostEstimate(flops=int(us * 4e3), bytes_accessed=int(us * 3e3), transcendentals=0)


def body(end, source, region, diri, rho_tab, cond_tab):
    n, radial = end.shape[1], end.shape[2]
    devices, rings = lax.axis_size("space"), lax.axis_size("tm")
    spacing = 2.0 * math.pi / (n * devices)
    tiles = n // 8
    part = tiles // 2 + 1

    end = end.reshape(2, tiles, 8, radial)
    source = source.reshape(2, 2, tiles, 8, radial)
    region = region.reshape(tiles, 8, radial)
    diri = diri.reshape(tiles, 8, radial)

    def f(*shape):
        return jax.ShapeDtypeStruct(shape + (radial,), F32)

    def buf(*shape):
        return pltpu.VMEM(shape + (radial,), F32)

    dma = pltpu.SemaphoreType.DMA
    ints = lambda *shape: pltpu.VMEM(shape + (radial,), jnp.int32)
    held = [pltpu.with_memory_space_constraint(v, pltpu.HBM) for v in (end, source, region, diri)]
    tabs = [pltpu.with_memory_space_constraint(v, pltpu.HBM) for v in (rho_tab, cond_tab)]
    tab_s = [pltpu.SMEM((rho_tab.shape[0],), F32)] * 2
    pack_a, pack_b, own = pl.pallas_call(
        pack_kernel,
        name="pack",
        out_shape=[f(16), f(8), f(6, 8)],
        in_specs=[ANY] * 4,
        out_specs=[VMEM] * 3,
        scratch_shapes=[buf(6, 8), ints(2, 8), dma((11,))],
        compiler_params=params(16),
        cost_estimate=cost(1.0),
    )(*held)

    up = [(t * devices + s, t * devices + (s + 1) % devices) for t in range(rings) for s in range(devices)]
    dn = [(b, a) for a, b in up]
    cross = lambda pairs: [(((a // devices + 1) % rings) * devices + a % devices, b) for a, b in pairs]
    both = ("tm", "space")
    back = [((t + 1) % rings, t) for t in range(rings)]
    got = lax.ppermute(own, "tm", back)
    up_a = lax.ppermute(pack_a, both, up)
    up_b = lax.ppermute(pack_b, both, cross(up))

    def chunk(base, lo, hi, after, packing):
        extra = [f(16), f(8)] if packing else []
        edge_s = [buf(6, 8), ints(2, 8), dma((8,))] if packing else []
        return pl.pallas_call(
            functools.partial(chunk_kernel, base, part, lo, hi, spacing),
            name="chunk",
            out_shape=[pltpu.VMEM((PLANES, part, 8, radial), F32), f(hi - lo, 8)] + extra,
            in_specs=[ANY] * 6 + [pl.BlockSpec(memory_space=pl.ANY)],
            out_specs=[VMEM] * (2 + len(extra)),
            scratch_shapes=edge_s + [
                ints(part, 8), ints(part, 8), buf(part + 2, 8), buf(part + 2, 8), buf(part, 8), buf(part, 8),
                buf(part, 8), buf(part + 2, 8), buf(part, 8), buf(4, 8),
            ] + tab_s + [dma((7,))],
            compiler_params=params(20),
            cost_estimate=cost(0.5),
        )(*tabs, *held, after)

    w1, c1 = chunk(0, 0, part - 1, own, False)
    w2, c2, dn_a, dn_b = chunk(tiles - part, 1, part, c1, True)
    c1 = lax.ppermute(c1, "tm", back)
    c2 = lax.ppermute(c2, "tm", back)
    dn_a = lax.ppermute(dn_a, both, dn)
    dn_b = lax.ppermute(dn_b, both, cross(dn))

    out, ends = pl.pallas_call(
        second_kernel,
        name="second",
        out_shape=[f(2, tiles, 8), f(2, 8)],
        in_specs=[VMEM, VMEM, ANY, ANY],
        out_specs=[ANY, VMEM],
        scratch_shapes=[buf(tiles + 2, 8)] * 2 + [buf(tiles, 8)] * 3 + [dma((4, 4))],
        compiler_params=params(20),
        cost_estimate=cost(0.5),
    )(w1, w2, *held[:2])

    for side, bulk, pa, pb in ((0, c1, up_a, up_b), (1, c2, dn_a, dn_b)):
        out = pl.pallas_call(
            functools.partial(edge_kernel, side, spacing),
            name="edge",
            out_shape=f(2, tiles, 8),
            in_specs=[ANY] * 6 + [VMEM] * 5 + [ANY],
            out_specs=ANY,
            scratch_shapes=[
                buf(3, 8), ints(2, 8), buf(2, 16), buf(2, 2, 16), ints(16), ints(16), buf(2, 8),
            ] + tab_s + [dma((10,))],
            input_output_aliases={11: 0},
            compiler_params=params(20),
            cost_estimate=cost(0.5),
        )(*tabs, *held, got, bulk, ends, pa, pb, out)
    return out.reshape(2, n, radial)


def solution(mesh):
    return jax.shard_map(
        body,
        mesh=mesh,
        in_specs=(
            P("tm", "space", None),
            P("tm", None, "space", None),
            P("space", None),
            P("space", None),
            P(),
            P(),
        ),
        out_specs=P("tm", "space", None),
        check_vma=False,
    )
```

```python
import functools
import math

import jax
import jax.numpy as jnp
from jax import lax
from jax.experimental import pallas as pl
from jax.experimental.pallas import tpu as pltpu
from jax.sharding import PartitionSpec as P

RELAX = 0.8
KEEP_SHARE = 0.2
F32 = jnp.float32
ANY = pl.BlockSpec(memory_space=pltpu.HBM)
VMEM = pl.BlockSpec(memory_space=pltpu.VMEM)
SMEM = pl.BlockSpec(memory_space=pltpu.SMEM)
PLANES = 7
LOOK, MAKE, GO = 17, 6, 17
LANES = 128


def tables(region, *names):
    low = (region & 1) != 0
    mid = (region & 2) != 0
    top = (region & 4) != 0
    found = []
    for t in names:
        pairs = [jnp.where(low, t[2 * k + 1], t[2 * k]) for k in range(4)]
        halves = [jnp.where(mid, pairs[2 * k + 1], pairs[2 * k]) for k in range(2)]
        found.append(jnp.where(top, halves[1], halves[0]))
    return found


def row_factors(rows, radial, spacing):
    lane = lax.broadcasted_iota(jnp.int32, (rows, radial), 1)
    position = lane.astype(F32)
    cycle = 1.0 + position * spacing
    outer = 0.5 * (1.0 + (position + 0.5) * spacing)
    inner = 0.5 * (1.0 + (position - 0.5) * spacing)
    return lane, cycle, 0.5 / cycle, outer, inner


def weight_planes(rho, rho_west, rho_east, cond, dirichlet, factors):
    lane, cycle, half_cycle, outer_f, inner_f = factors
    radial = rho.shape[1]
    first, final = lane == 0, lane == radial - 1
    up = jnp.where(final, rho, pltpu.roll(rho, radial - 1, 1))
    down = jnp.where(first, rho, pltpu.roll(rho, 1, 1))
    west = (rho + rho_west) * half_cycle
    east = (rho + rho_east) * half_cycle
    outer = (rho + up) * outer_f
    inner = (rho + down) * inner_f
    mass = cond * cycle
    diagonal = mass + west + east + outer + inner
    free = dirichlet == 0
    gain = jnp.where(free, RELAX / diagonal, 0.0)
    own = jnp.where(free, KEEP_SHARE, 0.0)
    outer_gain = jnp.where(final, 0.0, gain * outer)
    inner_gain = jnp.where(first, 0.0, gain * inner)
    return own, gain * west, gain * east, outer_gain, inner_gain, gain, gain * mass


def stencil(centre, west, east, w, right):
    radial = centre.shape[1]
    up = pltpu.roll(centre, radial - 1, 1)
    down = pltpu.roll(centre, 1, 1)
    return (w[0] * centre + w[1] * west) + (w[2] * east + w[3] * up) + (w[4] * down + right)


def copy_in(src, dst, sem):
    return pltpu.make_async_copy(src, dst, sem)


def each(lo, hi, work, group):
    group = min(group, hi - lo)
    groups = -(-(hi - lo) // group)

    def step(k, _):
        at = jnp.minimum(lo + k * group, hi - group)
        work([pl.multiple_of(8 * (at + m), 8) for m in range(group)])
        return 0

    lax.fori_loop(0, groups, step, 0)


def block(v):
    return pl.ds(v * LANES, LANES)


def load_blocks(src, x, rows, sem):
    return [copy_in(src.at[:, block(v)], x.at[v, pl.ds(8, rows), :], sem.at[v]) for v in range(x.shape[0])]


def seen(x, at):
    blocks = x.shape[0]
    lane = lax.broadcasted_iota(jnp.int32, (8, LANES), 1)
    c = [x[v, pl.ds(at + 8, 8), :] for v in range(blocks)]
    left = [pltpu.roll(u, LANES - 1, 1) for u in c]
    right = [pltpu.roll(u, 1, 1) for u in c]
    out = []
    for v in range(blocks):
        up = left[v] if v == blocks - 1 else jnp.where(lane == LANES - 1, left[v + 1], left[v])
        down = right[v] if v == 0 else jnp.where(lane == 0, right[v - 1], right[v])
        out.append((c[v], x[v, pl.ds(at + 7, 8), :], x[v, pl.ds(at + 9, 8), :], up, down))
    return out


def planes_of(v, blocks, near, cond, dirichlet, factors):
    rho, rho_west, rho_east, up, down = near
    cycle, half_cycle, outer_f, inner_f = factors
    lane = lax.broadcasted_iota(jnp.int32, (8, LANES), 1)
    if v == blocks - 1:
        up = jnp.where(lane == LANES - 1, rho, up)
    if v == 0:
        down = jnp.where(lane == 0, rho, down)
    west = (rho + rho_west) * half_cycle
    east = (rho + rho_east) * half_cycle
    outer = (rho + up) * outer_f
    inner = (rho + down) * inner_f
    mass = cond * cycle
    diagonal = mass + west + east + outer + inner
    free = dirichlet == 0
    gain = jnp.where(free, RELAX / diagonal, 0.0)
    own = jnp.where(free, KEEP_SHARE, 0.0)
    outer, inner = gain * outer, gain * inner
    if v == blocks - 1:
        outer = jnp.where(lane == LANES - 1, 0.0, outer)
    if v == 0:
        inner = jnp.where(lane == 0, 0.0, inner)
    return own, gain * west, gain * east, outer, inner, gain, gain * mass


def weights_loop(reg, diri, rho_s, cond_s, fac, w_out, rho_tab, cond_tab, tiles):
    blocks = rho_s.shape[0]

    def look(ats):
        for at in ats:
            for v in range(blocks):
                r, c = tables(reg[pl.ds(at, 8), block(v)], rho_tab, cond_tab)
                rho_s[v, pl.ds(at + 8, 8), :] = r
                cond_s[pl.ds(at, 8), block(v)] = c

    each(0, tiles, look, LOOK)

    def make(ats):
        for at in ats:
            near = seen(rho_s, at)
            for v in range(blocks):
                planes = planes_of(
                    v, blocks, near[v], cond_s[pl.ds(at, 8), block(v)], diri[pl.ds(at, 8), block(v)],
                    [fac[k, :, block(v)] for k in range(4)],
                )
                for k in range(PLANES):
                    w_out[k, pl.ds(at, 8), block(v)] = planes[k]

    each(0, tiles, make, MAKE)


def sweep(x, y, w, w_at, src, right, first, lo, hi, plain_at=None):
    blocks = x.shape[0]

    def go(ats):
        for at in ats:
            near = seen(x, at)
            wt = pl.multiple_of(at - 8 * w_at, 8)
            for v in range(blocks):
                c, west, east, up, down = near[v]
                p = [w[k, pl.ds(wt, 8), block(v)] for k in range(PLANES if first else 5)]
                if first:
                    b = p[5] * src[pl.ds(at, 8), block(v)] + p[6] * c
                    right[pl.ds(at, 8), block(v)] = b
                else:
                    b = right[pl.ds(at, 8), block(v)]
                new = (p[0] * c + p[1] * west) + (p[2] * east + p[3] * up) + (p[4] * down + b)
                if plain_at is None:
                    y[v, pl.ds(at + 8, 8), :] = new
                else:
                    y[pl.ds(pl.multiple_of(at - 8 * plain_at, 8), 8), block(v)] = new

    each(lo, hi, go, GO)


def own_kernel(rows, rho_tab, cond_tab, end, source, region, diri, own, reg1, dir1, splat, rt, ct, sems):
    last = end.shape[1] - 8
    copies = [copy_in(rho_tab, rt, sems.at[0]), copy_in(cond_tab, ct, sems.at[1])]
    for side, at in ((0, 0), (1, last)):
        for k, src in enumerate((end.at[0], source.at[0, 0], source.at[0, 1])):
            copies.append(copy_in(src.at[pl.ds(at, 8), :], own.at[3 * side + k], sems.at[2 + 3 * side + k]))
    copies.append(copy_in(region.at[pl.ds(0, rows), :], reg1, sems.at[8]))
    copies.append(copy_in(diri.at[pl.ds(0, rows), :], dir1, sems.at[9]))
    for c in copies:
        c.start()
    for c in copies[:2]:
        c.wait()
    for k in range(8):
        splat[k] = jnp.full((8, LANES), rt[k], F32)
        splat[8 + k] = jnp.full((8, LANES), ct[k], F32)
    for c in copies[2:]:
        c.wait()


def edge_loads(end, source, region, diri, side, buf, regs, sems):
    rows = pl.ds(side * (end.shape[1] - 8), 8)
    return [
        copy_in(end.at[1, rows, :], buf.at[0], sems.at[0]),
        copy_in(source.at[1, 0, rows, :], buf.at[1], sems.at[1]),
        copy_in(source.at[1, 1, rows, :], buf.at[2], sems.at[2]),
        copy_in(region.at[rows, :], regs.at[0], sems.at[3]),
        copy_in(diri.at[rows, :], regs.at[1], sems.at[4]),
    ]


def write_pack(buf, regs, got, out, side):
    pick = (lambda m: slice(0, m)) if side == 0 else (lambda m: slice(8 - m, 8))
    for at, parts in ((0, [buf[k] for k in range(3)]), (8, [got[3 * side + k] for k in range(3)])):
        out[at : at + 4, :] = parts[0][pick(4), :]
        out[at + 4 : at + 7, :] = parts[1][pick(3), :]
        out[at + 7 : at + 8, :] = parts[2][pick(1), :]
    out[16:20, :] = regs[0, pick(4), :].astype(F32)
    out[20:23, :] = regs[1, pick(3), :].astype(F32)
    out[23:24, :] = jnp.zeros((1, out.shape[1]), F32)


def pack_kernel(buf, regs, got, up):
    write_pack(buf, regs, got, up, 1)


def chunk_kernel(base, tiles, lo, hi, spacing, first, splat, reg_v, dir_v, end, source, region, diri, got, *refs):
    refs = refs if first else refs[1:]
    w_out, chunk, buf, regs = refs[:4]
    x, y, s0, s1, right, rho_s, cond_s, fac, sems, x_sems, edge_sems = refs[-11:]
    n, radial = end.shape[1:]
    rows = pl.ds(8 * base, 8 * tiles)
    state = load_blocks(end.at[0, rows], x, 8 * tiles, x_sems.at[0])
    later = [copy_in(source.at[0, 0, rows, :], s0, sems.at[0]), copy_in(source.at[0, 1, rows, :], s1, sems.at[1])]
    ahead = edge_loads(end, source, region, diri, 1 if first else 0, buf, regs, edge_sems)
    if first:
        reg2, dir2 = refs[4:6]
        ends = pl.ds(n - 8 * tiles, 8 * tiles)
        ahead += [copy_in(region.at[ends, :], reg2, sems.at[2]), copy_in(diri.at[ends, :], dir2, sems.at[3])]
    else:
        dn, x1, s10, s11 = refs[4:8]
        ahead += load_blocks(end.at[1], x1, n, x_sems.at[1])
        ahead += [copy_in(source.at[1, 0], s10, sems.at[2]), copy_in(source.at[1, 1], s11, sems.at[3])]
    for c in state + later + ahead:
        c.start()
    _, cycle, half, outer, inner = row_factors(8, radial, spacing)
    for k, f in enumerate((cycle, half, outer, inner)):
        fac[k] = f
    weights_loop(
        reg_v, dir_v, rho_s, cond_s, fac, w_out,
        [splat[k] for k in range(8)], [splat[8 + k] for k in range(8)], tiles,
    )
    for c in state + later[:1]:
        c.wait()
    sweep(x, y, w_out, 0, s0, right, True, 0, tiles)
    sweep(y, x, w_out, 0, None, right, False, 0, tiles)
    later[1].wait()
    sweep(x, y, w_out, 0, s1, right, True, 0, tiles)
    sweep(y, chunk, w_out, 0, None, right, False, lo, hi, lo)
    for c in ahead:
        c.wait()
    if not first:
        write_pack(buf, regs, got, dn, 0)


def second_kernel(w1, w2, x1, s0, s1, out, ends, x, y, right, plain, sems):
    rows = s0.shape[0]
    tiles = rows // 8
    half = tiles // 2
    skip = tiles - w2.shape[1] // 8

    def both(a, b, src, first, plain_at=None, after=None):
        for k, w, at in ((0, w1, 0), (1, w2, skip)):
            sweep(a, b, w, at, src, right, first, k * half, (k + 1) * half, plain_at)
            if after:
                after(k)

    def back(k):
        piece = pl.ds(8 * k * half, 8 * half)
        return copy_in(plain.at[piece, :], out.at[0, piece, :], sems.at[k])

    both(x1, y, s0, True)
    both(y, x, None, False)
    both(x, y, s1, True)
    both(y, plain, None, False, 0, lambda k: back(k).start())
    ends[0] = plain[0:8, :]
    ends[1] = plain[rows - 8 : rows, :]
    for k in range(2):
        back(k).wait()


def edge_kernel(
    side, spacing,
    splat, own, regs, got, bulk, ends, pack, _,
    out,
    xw, sw, rw, dw, tiles_out, sems,
):
    half, radial = bulk.shape
    rows = 2 * half
    at = pl.ds(side * (rows - 8), 8)
    moved = copy_in(
        bulk.at[pl.ds(8 - 8 * side, half - 8), :], out.at[1, pl.ds(half if side else 8, half - 8), :], sems.at[0]
    )
    moved.start()
    factors = row_factors(16, radial, spacing)
    zero = jnp.zeros((16, radial), F32)
    mine = 8 if side == 0 else 0
    halo = (lambda m: slice(8 - m, 8)) if side == 0 else (lambda m: slice(8, 8 + m))
    rw[...] = jnp.zeros((16, radial), jnp.int32)
    dw[...] = jnp.zeros((16, radial), jnp.int32)
    rw[halo(4), :] = pack[16:20, :].astype(jnp.int32)
    dw[halo(3), :] = pack[20:23, :].astype(jnp.int32)
    for p in range(2):
        xw[p] = zero
        sw[p, 0] = zero
        sw[p, 1] = zero
        xw[p, halo(4), :] = pack[8 * p : 8 * p + 4, :]
        sw[p, 0, halo(3), :] = pack[8 * p + 4 : 8 * p + 7, :]
        sw[p, 1, halo(1), :] = pack[8 * p + 7 : 8 * p + 8, :]
    xw[1, mine : mine + 8, :] = got[3 * side]
    sw[1, 0, mine : mine + 8, :] = got[3 * side + 1]
    sw[1, 1, mine : mine + 8, :] = got[3 * side + 2]
    rw[mine : mine + 8, :] = regs[0]
    dw[mine : mine + 8, :] = regs[1]
    xw[0, mine : mine + 8, :] = own[0]
    sw[0, 0, mine : mine + 8, :] = own[1]
    sw[0, 1, mine : mine + 8, :] = own[2]
    found = [
        tables(rw[:, block(v)], *[[jnp.concatenate([splat[8 * q + k]] * 2) for k in range(8)] for q in range(2)])
        for v in range(radial // LANES)
    ]
    rho = jnp.concatenate([u[0] for u in found], axis=1)
    cond = jnp.concatenate([u[1] for u in found], axis=1)
    w = weight_planes(rho, pltpu.roll(rho, 1, 0), pltpu.roll(rho, 15, 0), cond, dw[...], factors)
    state = [xw[0], xw[1]]
    for step in range(2):
        right = [w[5] * sw[p, step] + w[6] * state[p] for p in range(2)]
        for _ in range(2):
            state = [
                stencil(v, pltpu.roll(v, 1, 0), pltpu.roll(v, 15, 0), w, r) for v, r in zip(state, right)
            ]
    sub = lax.broadcasted_iota(jnp.int32, (8, radial), 0)
    edge = sub < 4 if side == 0 else sub >= 4
    stores = []
    for p, keep in ((0, ends[side]), (1, bulk[side * (half - 8) : side * (half - 8) + 8, :])):
        tiles_out[p] = jnp.where(edge, state[p][mine : mine + 8, :], keep)
        stores.append(copy_in(tiles_out.at[p], out.at[p, at, :], sems.at[1 + p]))
        stores[-1].start()
    for c in [moved] + stores:
        c.wait()


def params(mib):
    return pltpu.CompilerParams(vmem_limit_bytes=mib * 2**20)


def cost(us):
    return pl.CostEstimate(flops=int(us * 4e3), bytes_accessed=int(us * 3e3), transcendentals=0)


def body(end, source, region, diri, rho_tab, cond_tab):
    n, radial = end.shape[1], end.shape[2]
    devices, rings = lax.axis_size("space"), lax.axis_size("tm")
    spacing = 2.0 * math.pi / (n * devices)
    tiles = n // 8
    part = tiles // 2 + 1
    blocks = radial // LANES
    dma = pltpu.SemaphoreType.DMA

    def f(*shape):
        return jax.ShapeDtypeStruct(shape + (radial,), F32)

    def buf(*shape):
        return pltpu.VMEM(shape + (radial,), F32)

    def ints(*shape):
        return pltpu.VMEM(shape + (radial,), jnp.int32)

    def cut(rows):
        return pltpu.VMEM((blocks, rows + 16, LANES), F32)

    held = [pltpu.with_memory_space_constraint(v, pltpu.HBM) for v in (end, source, region, diri)]
    tabs = [pltpu.with_memory_space_constraint(v, pltpu.HBM) for v in (rho_tab, cond_tab)]
    tab_s = [pltpu.SMEM((rho_tab.shape[0],), F32)] * 2
    edge_o = [buf(3, 8), ints(2, 8)]

    up = [(s, (s + 1) % devices) for s in range(devices)]
    down = [(b, a) for a, b in up]
    back = [((t + 1) % rings, t) for t in range(rings)]

    rows = 8 * part
    own, reg1, dir1, splat = pl.pallas_call(
        functools.partial(own_kernel, rows),
        name="own",
        out_shape=[f(6, 8), ints(rows), ints(rows), pltpu.VMEM((16, 8, LANES), F32)],
        in_specs=[ANY] * 6,
        out_specs=[VMEM] * 4,
        scratch_shapes=tab_s + [dma((10,))],
        compiler_params=params(16),
        cost_estimate=cost(1),
    )(*tabs, *held)
    got = lax.ppermute(own, "tm", back)

    def chunk(base, lo, hi, reg, dirs, got, extra):
        return pl.pallas_call(
            functools.partial(chunk_kernel, base, part, lo, hi, spacing, base == 0),
            name="chunk",
            out_shape=[pltpu.VMEM((PLANES, rows, radial), F32), f(8 * (hi - lo))] + edge_o + extra,
            in_specs=[VMEM] * 3 + [ANY] * 4 + [VMEM] * len(got),
            out_specs=[VMEM] * (4 + len(extra)),
            scratch_shapes=[cut(rows), cut(rows), buf(rows), buf(rows), buf(rows), cut(rows), buf(rows), buf(4, 8)]
            + [dma((4,)), dma((2, blocks)), dma((5,))],
            compiler_params=params(20),
            cost_estimate=cost(1),
        )(splat, reg, dirs, *held, *got)

    w1, c1, buf1, regs1, reg2, dir2 = chunk(0, 0, part - 1, reg1, dir1, [own], [ints(rows), ints(rows)])
    pack = pl.pallas_call(
        pack_kernel,
        name="pack",
        out_shape=f(24),
        in_specs=[VMEM] * 3,
        out_specs=VMEM,
        compiler_params=params(16),
        cost_estimate=cost(1),
    )(buf1, regs1, got)
    w2, c2, buf0, regs0, dn, x1, s10, s11 = chunk(
        tiles - part, 1, part, reg2, dir2, [got, pack], [f(24), cut(n), buf(n), buf(n)]
    )
    c1 = lax.ppermute(c1, "tm", back)
    c2 = lax.ppermute(c2, "tm", back)
    pack = lax.ppermute(pack, "space", up)
    dn = lax.ppermute(dn, "space", down)

    out, ends = pl.pallas_call(
        second_kernel,
        name="second",
        out_shape=[f(2, n), f(2, 8)],
        in_specs=[VMEM] * 5,
        out_specs=[ANY, VMEM],
        scratch_shapes=[cut(n), cut(n), buf(n), buf(n), dma((2,))],
        compiler_params=params(20),
        cost_estimate=cost(1),
    )(w1, w2, x1, s10, s11)

    for side, bulk, halo, edge in ((0, c1, pack, (buf0, regs0)), (1, c2, dn, (buf1, regs1))):
        out = pl.pallas_call(
            functools.partial(edge_kernel, side, spacing),
            name="edge",
            out_shape=f(2, n),
            in_specs=[VMEM] * 7 + [ANY],
            out_specs=ANY,
            scratch_shapes=[buf(2, 16), buf(2, 2, 16), ints(16), ints(16), buf(2, 8), dma((3,))],
            input_output_aliases={7: 0},
            compiler_params=params(20),
            cost_estimate=cost(100 if side == 0 else 1),
        )(splat, *edge, got, bulk, ends, halo, out)
    return out


def solution(mesh):
    return jax.shard_map(
        body,
        mesh=mesh,
        in_specs=(
            P("tm", "space", None),
            P("tm", None, "space", None),
            P("space", None),
            P("space", None),
            P(),
            P(),
        ),
        out_specs=P("tm", "space", None),
        check_vma=False,
    )
```

```python
import functools
import math

import jax
import jax.numpy as jnp
from jax import lax
from jax.experimental import pallas as pl
from jax.experimental.pallas import tpu as pltpu
from jax.sharding import PartitionSpec as P

RELAX = 0.8
KEEP_SHARE = 0.2
F32 = jnp.float32
ANY = pl.BlockSpec(memory_space=pltpu.HBM)
VMEM = pl.BlockSpec(memory_space=pltpu.VMEM)
SMEM = pl.BlockSpec(memory_space=pltpu.SMEM)
PLANES = 7
LOOK, MAKE, GO = 9, 6, 17
LANES = 128


def tables(region, *names):
    low = (region & 1) != 0
    mid = (region & 2) != 0
    top = (region & 4) != 0
    found = []
    for t in names:
        pairs = [jnp.where(low, t[2 * k + 1], t[2 * k]) for k in range(4)]
        halves = [jnp.where(mid, pairs[2 * k + 1], pairs[2 * k]) for k in range(2)]
        found.append(jnp.where(top, halves[1], halves[0]))
    return found


def row_factors(rows, radial, spacing):
    lane = lax.broadcasted_iota(jnp.int32, (rows, radial), 1)
    position = lane.astype(F32)
    cycle = 1.0 + position * spacing
    outer = 0.5 * (1.0 + (position + 0.5) * spacing)
    inner = 0.5 * (1.0 + (position - 0.5) * spacing)
    return lane, cycle, 0.5 / cycle, outer, inner


def weight_planes(rho, rho_west, rho_east, cond, dirichlet, factors):
    lane, cycle, half_cycle, outer_f, inner_f = factors
    radial = rho.shape[1]
    first, final = lane == 0, lane == radial - 1
    up = jnp.where(final, rho, pltpu.roll(rho, radial - 1, 1))
    down = jnp.where(first, rho, pltpu.roll(rho, 1, 1))
    west = (rho + rho_west) * half_cycle
    east = (rho + rho_east) * half_cycle
    outer = (rho + up) * outer_f
    inner = (rho + down) * inner_f
    mass = cond * cycle
    diagonal = mass + west + east + outer + inner
    free = dirichlet == 0
    gain = jnp.where(free, RELAX / diagonal, 0.0)
    own = jnp.where(free, KEEP_SHARE, 0.0)
    outer_gain = jnp.where(final, 0.0, gain * outer)
    inner_gain = jnp.where(first, 0.0, gain * inner)
    return own, gain * west, gain * east, outer_gain, inner_gain, gain, gain * mass


def stencil(centre, west, east, w, right):
    radial = centre.shape[1]
    up = pltpu.roll(centre, radial - 1, 1)
    down = pltpu.roll(centre, 1, 1)
    return (w[0] * centre + w[1] * west) + (w[2] * east + w[3] * up) + (w[4] * down + right)


def copy_in(src, dst, sem):
    return pltpu.make_async_copy(src, dst, sem)


def each(lo, hi, work, group):
    group = min(group, hi - lo)
    groups = -(-(hi - lo) // group)

    def step(k, _):
        at = jnp.minimum(lo + k * group, hi - group)
        work([pl.multiple_of(8 * (at + m), 8) for m in range(group)])
        return 0

    lax.fori_loop(0, groups, step, 0)


def block(v):
    return pl.ds(v * LANES, LANES)


def load_blocks(src, x, rows, sem):
    return [copy_in(src.at[:, block(v)], x.at[v, pl.ds(8, rows), :], sem.at[v]) for v in range(x.shape[0])]


def seen(x, at):
    blocks = x.shape[0]
    lane = lax.broadcasted_iota(jnp.int32, (8, LANES), 1)
    c = [x[v, pl.ds(at + 8, 8), :] for v in range(blocks)]
    left = [pltpu.roll(u, LANES - 1, 1) for u in c]
    right = [pltpu.roll(u, 1, 1) for u in c]
    out = []
    for v in range(blocks):
        up = left[v] if v == blocks - 1 else jnp.where(lane == LANES - 1, left[v + 1], left[v])
        down = right[v] if v == 0 else jnp.where(lane == 0, right[v - 1], right[v])
        out.append((c[v], x[v, pl.ds(at + 7, 8), :], x[v, pl.ds(at + 9, 8), :], up, down))
    return out


def planes_of(v, blocks, near, cond, dirichlet, factors):
    rho, rho_west, rho_east, up, down = near
    cycle, half_cycle, outer_f, inner_f = factors
    lane = lax.broadcasted_iota(jnp.int32, (8, LANES), 1)
    if v == blocks - 1:
        up = jnp.where(lane == LANES - 1, rho, up)
    if v == 0:
        down = jnp.where(lane == 0, rho, down)
    west = (rho + rho_west) * half_cycle
    east = (rho + rho_east) * half_cycle
    outer = (rho + up) * outer_f
    inner = (rho + down) * inner_f
    mass = cond * cycle
    diagonal = mass + west + east + outer + inner
    free = dirichlet == 0
    gain = jnp.where(free, RELAX / diagonal, 0.0)
    own = jnp.where(free, KEEP_SHARE, 0.0)
    outer, inner = gain * outer, gain * inner
    if v == blocks - 1:
        outer = jnp.where(lane == LANES - 1, 0.0, outer)
    if v == 0:
        inner = jnp.where(lane == 0, 0.0, inner)
    return own, gain * west, gain * east, outer, inner, gain, gain * mass


def weights_loop(reg, diri, rho_s, cond_s, fac, w_out, rho_tab, cond_tab, tiles):
    blocks = rho_s.shape[0]

    def look(ats):
        for at in ats:
            for v in range(blocks):
                r, c = tables(reg[pl.ds(at, 8), block(v)], rho_tab, cond_tab)
                rho_s[v, pl.ds(at + 8, 8), :] = r
                cond_s[pl.ds(at, 8), block(v)] = c

    each(0, tiles, look, LOOK)

    def make(ats):
        for at in ats:
            near = seen(rho_s, at)
            for v in range(blocks):
                planes = planes_of(
                    v, blocks, near[v], cond_s[pl.ds(at, 8), block(v)], diri[pl.ds(at, 8), block(v)],
                    [fac[k, :, block(v)] for k in range(4)],
                )
                for k in range(PLANES):
                    w_out[k, pl.ds(at, 8), block(v)] = planes[k]

    each(0, tiles, make, MAKE)


def sweep(x, y, w, w_at, src, right, first, lo, hi, plain_at=None):
    blocks = x.shape[0]

    def go(ats):
        for at in ats:
            near = seen(x, at)
            wt = pl.multiple_of(at - 8 * w_at, 8)
            for v in range(blocks):
                c, west, east, up, down = near[v]
                p = [w[k, pl.ds(wt, 8), block(v)] for k in range(PLANES if first else 5)]
                if first:
                    b = p[5] * src[pl.ds(at, 8), block(v)] + p[6] * c
                    right[pl.ds(at, 8), block(v)] = b
                else:
                    b = right[pl.ds(at, 8), block(v)]
                new = (p[0] * c + p[1] * west) + (p[2] * east + p[3] * up) + (p[4] * down + b)
                if plain_at is None:
                    y[v, pl.ds(at + 8, 8), :] = new
                else:
                    y[pl.ds(pl.multiple_of(at - 8 * plain_at, 8), 8), block(v)] = new

    each(lo, hi, go, GO)


def own_kernel(rows, rho_tab, cond_tab, end, source, region, diri, own, reg1, dir1, splat, rt, ct, sems):
    last = end.shape[1] - 8
    copies = [copy_in(rho_tab, rt, sems.at[0]), copy_in(cond_tab, ct, sems.at[1])]
    for side, at in ((0, 0), (1, last)):
        for k, src in enumerate((end.at[0], source.at[0, 0], source.at[0, 1])):
            copies.append(copy_in(src.at[pl.ds(at, 8), :], own.at[3 * side + k], sems.at[2 + 3 * side + k]))
    copies.append(copy_in(region.at[pl.ds(0, rows), :], reg1, sems.at[8]))
    copies.append(copy_in(diri.at[pl.ds(0, rows), :], dir1, sems.at[9]))
    for c in copies:
        c.start()
    for c in copies[:2]:
        c.wait()
    for k in range(8):
        splat[k] = jnp.full((8, LANES), rt[k], F32)
        splat[8 + k] = jnp.full((8, LANES), ct[k], F32)
    for c in copies[2:]:
        c.wait()


def edge_loads(end, source, region, diri, side, buf, regs, sems):
    rows = pl.ds(side * (end.shape[1] - 8), 8)
    return [
        copy_in(end.at[1, rows, :], buf.at[0], sems.at[0]),
        copy_in(source.at[1, 0, rows, :], buf.at[1], sems.at[1]),
        copy_in(source.at[1, 1, rows, :], buf.at[2], sems.at[2]),
        copy_in(region.at[rows, :], regs.at[0], sems.at[3]),
        copy_in(diri.at[rows, :], regs.at[1], sems.at[4]),
    ]


def write_pack(buf, regs, got, out, side):
    pick = (lambda m: slice(0, m)) if side == 0 else (lambda m: slice(8 - m, 8))
    for at, parts in ((0, [buf[k] for k in range(3)]), (8, [got[3 * side + k] for k in range(3)])):
        out[at : at + 4, :] = parts[0][pick(4), :]
        out[at + 4 : at + 7, :] = parts[1][pick(3), :]
        out[at + 7 : at + 8, :] = parts[2][pick(1), :]
    out[16:20, :] = regs[0, pick(4), :].astype(F32)
    out[20:23, :] = regs[1, pick(3), :].astype(F32)
    out[23:24, :] = jnp.zeros((1, out.shape[1]), F32)


def pack_kernel(buf, regs, got, up):
    write_pack(buf, regs, got, up, 1)


def chunk_kernel(base, tiles, lo, hi, spacing, first, splat, reg_v, dir_v, end, source, region, diri, got, *refs):
    refs = refs if first else refs[1:]
    w_out, chunk, buf, regs = refs[:4]
    x, y, s0, s1, right, rho_s, cond_s, fac, sems, x_sems, edge_sems = refs[-11:]
    n, radial = end.shape[1:]
    rows = pl.ds(8 * base, 8 * tiles)
    state = load_blocks(end.at[0, rows], x, 8 * tiles, x_sems.at[0])
    later = [copy_in(source.at[0, 0, rows, :], s0, sems.at[0]), copy_in(source.at[0, 1, rows, :], s1, sems.at[1])]
    ahead = edge_loads(end, source, region, diri, 1 if first else 0, buf, regs, edge_sems)
    if first:
        reg2, dir2 = refs[4:6]
        ends = pl.ds(n - 8 * tiles, 8 * tiles)
        ahead += [copy_in(region.at[ends, :], reg2, sems.at[2]), copy_in(diri.at[ends, :], dir2, sems.at[3])]
    else:
        dn, x1, s10, s11 = refs[4:8]
        ahead += load_blocks(end.at[1], x1, n, x_sems.at[1])
        ahead += [copy_in(source.at[1, 0], s10, sems.at[2]), copy_in(source.at[1, 1], s11, sems.at[3])]
    for c in state + later + ahead:
        c.start()
    _, cycle, half, outer, inner = row_factors(8, radial, spacing)
    for k, f in enumerate((cycle, half, outer, inner)):
        fac[k] = f
    weights_loop(
        reg_v, dir_v, rho_s, cond_s, fac, w_out,
        [splat[k] for k in range(8)], [splat[8 + k] for k in range(8)], tiles,
    )
    for c in state + later[:1]:
        c.wait()
    sweep(x, y, w_out, 0, s0, right, True, 0, tiles)
    sweep(y, x, w_out, 0, None, right, False, 0, tiles)
    later[1].wait()
    sweep(x, y, w_out, 0, s1, right, True, 0, tiles)
    sweep(y, chunk, w_out, 0, None, right, False, lo, hi, lo)
    for c in ahead:
        c.wait()
    if not first:
        write_pack(buf, regs, got, dn, 0)


def second_kernel(w1, w2, x1, s0, s1, out, ends, x, y, right, plain, sems):
    rows = s0.shape[0]
    tiles = rows // 8
    half = tiles // 2
    skip = tiles - w2.shape[1] // 8

    def both(a, b, src, first, plain_at=None, after=None):
        for k, w, at in ((0, w1, 0), (1, w2, skip)):
            sweep(a, b, w, at, src, right, first, k * half, (k + 1) * half, plain_at)
            if after:
                after(k)

    def back(k):
        piece = pl.ds(8 * k * half, 8 * half)
        return copy_in(plain.at[piece, :], out.at[0, piece, :], sems.at[k])

    both(x1, y, s0, True)
    both(y, x, None, False)
    both(x, y, s1, True)
    both(y, plain, None, False, 0, lambda k: back(k).start())
    ends[0] = plain[0:8, :]
    ends[1] = plain[rows - 8 : rows, :]
    for k in range(2):
        back(k).wait()


def edge_kernel(
    spacing, splat, own0, regs0, own1, regs1, got, ends, from_up, from_down, *refs
):
    *bulk, _, out, xw, sw, rw, dw, tiles_out, sems = refs
    rows, radial = out.shape[1:]
    moved = []
    row = 0
    for k, b in enumerate(bulk):
        skip = 8 if k == 0 else 0
        size = b.shape[0] - skip - (8 if k + 1 == len(bulk) else 0)
        moved.append(copy_in(b.at[pl.ds(skip, size), :], out.at[1, pl.ds(row + skip, size), :], sems.at[4 + k]))
        row += b.shape[0]
    for c in moved:
        c.start()
    factors = row_factors(16, radial, spacing)
    zero = jnp.zeros((16, radial), F32)
    weights, state = [], []
    for side, own, regs, pack in ((0, own0, regs0, from_up), (1, own1, regs1, from_down)):
        mine = 8 if side == 0 else 0
        halo = (lambda m: slice(8 - m, 8)) if side == 0 else (lambda m: slice(8, 8 + m))
        rw[side] = jnp.zeros((16, radial), jnp.int32)
        dw[side] = jnp.zeros((16, radial), jnp.int32)
        rw[side, halo(4), :] = pack[16:20, :].astype(jnp.int32)
        dw[side, halo(3), :] = pack[20:23, :].astype(jnp.int32)
        rw[side, mine : mine + 8, :] = regs[0]
        dw[side, mine : mine + 8, :] = regs[1]
        for p in range(2):
            xw[side, p] = zero
            sw[side, p, 0] = zero
            sw[side, p, 1] = zero
            xw[side, p, halo(4), :] = pack[8 * p : 8 * p + 4, :]
            sw[side, p, 0, halo(3), :] = pack[8 * p + 4 : 8 * p + 7, :]
            sw[side, p, 1, halo(1), :] = pack[8 * p + 7 : 8 * p + 8, :]
            parts = [own[k] for k in range(3)] if p == 0 else [got[3 * side + k] for k in range(3)]
            xw[side, p, mine : mine + 8, :] = parts[0]
            sw[side, p, 0, mine : mine + 8, :] = parts[1]
            sw[side, p, 1, mine : mine + 8, :] = parts[2]
        found = [
            tables(
                rw[side, :, block(v)],
                *[[jnp.concatenate([splat[8 * q + k]] * 2) for k in range(8)] for q in range(2)],
            )
            for v in range(radial // LANES)
        ]
        rho = jnp.concatenate([u[0] for u in found], axis=1)
        cond = jnp.concatenate([u[1] for u in found], axis=1)
        weights.append(
            weight_planes(rho, pltpu.roll(rho, 1, 0), pltpu.roll(rho, 15, 0), cond, dw[side], factors)
        )
        state += [(side, p, xw[side, p]) for p in range(2)]
    for step in range(2):
        right = [weights[side][5] * sw[side, p, step] + weights[side][6] * v for side, p, v in state]
        for _ in range(2):
            state = [
                (side, p, stencil(v, pltpu.roll(v, 1, 0), pltpu.roll(v, 15, 0), weights[side], r))
                for (side, p, v), r in zip(state, right)
            ]
    sub = lax.broadcasted_iota(jnp.int32, (8, radial), 0)
    stores = []
    for k, (side, p, v) in enumerate(state):
        mine = 8 if side == 0 else 0
        if p == 0:
            keep = ends[side]
        else:
            keep = bulk[0][0:8, :] if side == 0 else bulk[-1][bulk[-1].shape[0] - 8 :, :]
        edge = sub < 4 if side == 0 else sub >= 4
        tiles_out[k] = jnp.where(edge, v[mine : mine + 8, :], keep)
        stores.append(
            copy_in(tiles_out.at[k], out.at[p, pl.ds(side * (rows - 8), 8), :], sems.at[k])
        )
        stores[-1].start()
    for c in moved + stores:
        c.wait()


def params(mib):
    return pltpu.CompilerParams(vmem_limit_bytes=mib * 2**20)


def cost(us):
    return pl.CostEstimate(flops=int(us * 4e3), bytes_accessed=int(us * 3e3), transcendentals=0)


def body(end, source, region, diri, rho_tab, cond_tab):
    n, radial = end.shape[1], end.shape[2]
    devices, rings = lax.axis_size("space"), lax.axis_size("tm")
    spacing = 2.0 * math.pi / (n * devices)
    tiles = n // 8
    part = tiles // 2 + 1
    blocks = radial // LANES
    dma = pltpu.SemaphoreType.DMA

    def f(*shape):
        return jax.ShapeDtypeStruct(shape + (radial,), F32)

    def buf(*shape):
        return pltpu.VMEM(shape + (radial,), F32)

    def ints(*shape):
        return pltpu.VMEM(shape + (radial,), jnp.int32)

    def cut(rows):
        return pltpu.VMEM((blocks, rows + 16, LANES), F32)

    held = [pltpu.with_memory_space_constraint(v, pltpu.HBM) for v in (end, source, region, diri)]
    tabs = [pltpu.with_memory_space_constraint(v, pltpu.HBM) for v in (rho_tab, cond_tab)]
    tab_s = [pltpu.SMEM((rho_tab.shape[0],), F32)] * 2
    edge_o = [buf(3, 8), ints(2, 8)]

    up = [(s, (s + 1) % devices) for s in range(devices)]
    down = [(b, a) for a, b in up]
    back = [((t + 1) % rings, t) for t in range(rings)]

    rows = 8 * part
    own, reg1, dir1, splat = pl.pallas_call(
        functools.partial(own_kernel, rows),
        name="own",
        out_shape=[f(6, 8), ints(rows), ints(rows), pltpu.VMEM((16, 8, LANES), F32)],
        in_specs=[ANY] * 6,
        out_specs=[VMEM] * 4,
        scratch_shapes=tab_s + [dma((10,))],
        compiler_params=params(10),
        cost_estimate=cost(1),
    )(*tabs, *held)
    got = lax.ppermute(own, "tm", back)

    def chunk(base, lo, hi, reg, dirs, got, extra):
        return pl.pallas_call(
            functools.partial(chunk_kernel, base, part, lo, hi, spacing, base == 0),
            name="chunk",
            out_shape=[pltpu.VMEM((PLANES, rows, radial), F32), f(8 * (hi - lo))] + edge_o + extra,
            in_specs=[VMEM] * 3 + [ANY] * 4 + [VMEM] * len(got),
            out_specs=[VMEM] * (4 + len(extra)),
            scratch_shapes=[cut(rows), cut(rows), buf(rows), buf(rows), buf(rows), cut(rows), buf(rows), buf(4, 8)]
            + [dma((4,)), dma((2, blocks)), dma((5,))],
            compiler_params=params(10),
            cost_estimate=cost(1),
        )(splat, reg, dirs, *held, *got)

    w1, c1, buf1, regs1, reg2, dir2 = chunk(0, 0, part - 1, reg1, dir1, [own], [ints(rows), ints(rows)])
    pack = pl.pallas_call(
        pack_kernel,
        name="pack",
        out_shape=f(24),
        in_specs=[VMEM] * 3,
        out_specs=VMEM,
        compiler_params=params(10),
        cost_estimate=cost(1),
    )(buf1, regs1, got)
    w2, c2, buf0, regs0, dn, x1, s10, s11 = chunk(
        tiles - part, 1, part, reg2, dir2, [got, pack], [f(24), cut(n), buf(n), buf(n)]
    )
    c1 = lax.ppermute(c1, "tm", back)
    c2 = lax.ppermute(c2, "tm", back)
    pack = lax.ppermute(pack, "space", up)
    dn = lax.ppermute(dn, "space", down)

    out, ends = pl.pallas_call(
        second_kernel,
        name="second",
        out_shape=[f(2, n), f(2, 8)],
        in_specs=[VMEM] * 5,
        out_specs=[ANY, VMEM],
        scratch_shapes=[cut(n), cut(n), buf(n), buf(n), dma((2,))],
        compiler_params=params(10),
        cost_estimate=cost(1),
    )(w1, w2, x1, s10, s11)

    bulk = [c1, c2]
    return pl.pallas_call(
        functools.partial(edge_kernel, spacing),
        name="edge",
        out_shape=f(2, n),
        in_specs=[VMEM] * (9 + len(bulk)) + [ANY],
        out_specs=ANY,
        scratch_shapes=[buf(2, 2, 16), buf(2, 2, 2, 16), ints(2, 16), ints(2, 16), buf(4, 8), dma((4 + len(bulk),))],
        input_output_aliases={9 + len(bulk): 0},
        compiler_params=params(10),
        cost_estimate=cost(1),
    )(splat, buf0, regs0, buf1, regs1, got, ends, pack, dn, *bulk, out)


def solution(mesh):
    return jax.shard_map(
        body,
        mesh=mesh,
        in_specs=(
            P("tm", "space", None),
            P("tm", None, "space", None),
            P("space", None),
            P("space", None),
            P(),
            P(),
        ),
        out_specs=P("tm", "space", None),
        check_vma=False,
    )
```
